256 devices in a mesh: ctx: 32 (over y, x, core), head: 8 (over z).
Axes of the slice: x: 4, y: 4, z: 8, core: 2. Of those that a mesh axis runs over, the one named last changes fastest.
Arguments:
- query_key: bfloat16 [16384, 1024], P('ctx', 'head'), may hold values from -6 to 6
- values: bfloat16 [16384, 4096], P('ctx', 'head'), may hold values from -6 to 6
- out_grad: bfloat16 [16384, 4096], P('ctx', 'head'), may hold values from -6 to 6
- out_weight: bfloat16 [4096, 4096], P('head'), may hold values from -0.09375 to 0.09375
- doc_lengths: int32 [128], replicated, may hold values from 1 to 2048, 16384 in all
Outputs:
- qk_grad: bfloat16 [16384, 1024], P('ctx', 'head')
- value_grad: bfloat16 [16384, 4096], P('ctx', 'head')
- proj_grad: float32 [4096, 4096], P('head', 'ctx')
The draws below stay inside these ranges and needn't reach their ends.
Inputs may be any that keep to these rules, and one draw needn't show every extreme that they name: `doc_lengths`: the documents fill all 16384 positions in order; the longest has exactly 2048 tokens.
All inputs are finite; a program needn't handle non-finite values.
Results may differ from the reference program's by a relative error of at most 0.0068.
Values may be sent and summed in bfloat16 or wider, within the bound.
No kernel may reach another device: no remote copies, remote signals or barrier semaphores. Data moves between devices by JAX's collectives and lax.ppermute only.
A program may use at most 128 MiB of HBM per device.

```python
import math
import jax
import jax.numpy as jnp
import numpy as np
from jax import lax

D = 4096
H = 32
HEAD = 128
QK = 16
FEAT = 273
T_DEV = 512
NTOK = 16384
NDOC = 128
DOC_MOST = 2048
N_CTX = 32


def raised(values, own_key, source, target, blocks, factor):
    owner, partner = [(jnp.arange(values.shape[axis_at]) // (values.shape[axis_at] // blocks)).reshape([-1 if axis == axis_at else 1 for axis in range(values.ndim)]) for axis_at in (source, target)]
    chosen = jax.random.permutation(own_key, blocks)[partner]
    strong = (owner == chosen) | (owner == (partner + blocks // 2) % blocks)
    return jnp.where(strong, factor * values, values)


def block_scale(rng, dims, cuts, smallest, high):
    def one(dim, parts):
        steps = jax.random.uniform(jax.random.fold_in(jax.random.fold_in(rng, 6), dim), (parts,), jnp.float32, smallest / len(cuts), high / len(cuts))
        return jnp.repeat(jnp.exp(steps), dims[dim] // parts).reshape((-1,) + (1,) * (len(dims) - dim - 1))

    factor_of = one(*cuts[0])
    for cut in cuts[1:]:
        factor_of = factor_of * one(*cut)
    return factor_of


def profile(count, total, reach, skew):
    portions = [(1 << 20) // math.isqrt(grade ** skew) + 1 for grade in range(2, count + 1)]
    surplus, holding = total - reach - (count - 1), [1] * (count - 1)
    while surplus > 0:
        movable = [i for i in range(count - 1) if holding[i] < reach]
        mass, left = sum([portions[i] for i in movable]), surplus
        for i in movable:
            more = min(reach - holding[i], max(1, left * portions[i] // mass), surplus)
            holding[i] = holding[i] + more
            surplus = surplus - more
    return np.array([reach] + holding)


def ragged_sizes(own_key, amount, total, bound, slope):
    if amount == 2:
        one = jax.random.randint(own_key, (), max(1, total - bound), min(bound, total - 1) + 1)
        return jnp.stack([one, total - one])
    lengths = jnp.asarray(profile(amount, total, bound, slope), jnp.int32)
    pairs = (amount - 1) // 2
    source_of, taker = lengths[1:1 + 2 * pairs:2], lengths[2:2 + 2 * pairs:2]
    slack = jnp.minimum(source_of - 1, bound - taker)
    passed = jax.random.randint(jax.random.fold_in(own_key, 1), (pairs,), 0, 1 << 20) % (slack + 1)
    lengths = lengths.at[1:1 + 2 * pairs:2].set(source_of - passed).at[2:2 + 2 * pairs:2].set(taker + passed)
    return lengths[jax.random.permutation(jax.random.fold_in(own_key, 2), amount)]


def noise(key, dims, width, reach, pieces=(), kind=jnp.bfloat16):
    values = jax.random.normal(key, dims, jnp.float32) * width
    if len(pieces) > 0:
        values = block_scale(key, dims, pieces, -0.22, 0.18) * values
    return jnp.clip(values, min=-reach, max=reach).astype(kind)


def gaussian_with(stream_key, extent, deviation, limit, shards, heavy, held_as=jnp.bfloat16):
    entries = deviation * jax.random.normal(stream_key, extent, jnp.float32)
    if shards:
        entries = entries * block_scale(stream_key, extent, shards, -0.22, 0.18)
    return jnp.clip(raised(entries, jax.random.fold_in(stream_key, 3), *heavy), -limit, limit).astype(held_as)


def setup_inputs(seed: int = 0) -> dict:
    seeds = jax.random.split(jax.random.key(seed), 6)
    return {
        "query_key": noise(seeds[0], (NTOK, H * 2 * QK), 1.0, 6.0, ((0, 32), (1, 8))),
        "values": noise(seeds[1], (NTOK, H * HEAD), 1.0, 6.0, ((0, 32), (1, 8))),
        "out_grad": gaussian_with(seeds[2], (NTOK, D), 1.0, 6.0, ((0, 32), (1, 8)), (0, 1, 32, 2.75)),
        "out_weight": noise(seeds[3], (H * HEAD, D), (H * HEAD) ** -0.5, 0.09375, ((0, 8),)),
        "doc_lengths": ragged_sizes(seeds[4], NDOC, NTOK, DOC_MOST, 2).astype(jnp.int32),
    }


quad_scale = 0.25 / math.sqrt(2.0)
highest = lax.Precision.HIGHEST

def rounded(array):
    return lax.optimization_barrier(array.astype(jnp.bfloat16)).astype(jnp.float32)

def features(points):
    feat_width = points.shape[-1]
    constant = jnp.ones(points.shape[:-1] + (1,), jnp.float32)
    products = (points[..., :, None] * points[..., None, :]).reshape(points.shape[:-1] + (feat_width * feat_width,))
    return jnp.concatenate([constant, points * 0.5, products * quad_scale], axis=-1)

def feature_grad(grad_feat, points):
    feat_width = points.shape[-1]
    linear = grad_feat[..., 1:1 + feat_width] * 0.5
    square = grad_feat[..., 1 + feat_width:].reshape(points.shape[:-1] + (feat_width, feat_width))
    paired = square + jnp.swapaxes(square, -1, -2)
    return linear + quad_scale * lax.optimization_barrier(jnp.sum(paired * points[..., None, :], axis=-1))

def segment_ids(doc_lengths, positions):
    starts = (jnp.cumsum(doc_lengths, dtype=jnp.int32) - doc_lengths).astype(jnp.int32)
    return lax.optimization_barrier(jnp.sum((starts[None, :] <= positions[:, None]).astype(jnp.int32), axis=1)).astype(jnp.int32) - 1

def reference(query_key, values, out_grad, out_weight, doc_lengths):
    positions = jnp.arange(NTOK, dtype=jnp.int32)
    segment = segment_ids(doc_lengths, positions).reshape(N_CTX, T_DEV)
    previous = segment_ids(doc_lengths, positions - 1).reshape(N_CTX, T_DEV)
    open_before = previous[:, 0]
    open_after = segment[:, T_DEV - 1]
    restart = (open_after != open_before).astype(jnp.float32)
    carried = (segment == open_before[:, None]).astype(jnp.float32)
    ending = (segment == open_after[:, None]).astype(jnp.float32)
    paired = query_key.reshape(N_CTX, T_DEV, H, 2, QK).transpose(0, 2, 3, 1, 4)
    value_rows = values.reshape(N_CTX, T_DEV, H, HEAD).transpose(0, 2, 1, 3)
    upstream_all = jnp.dot(out_grad, out_weight.T, preferred_element_type=jnp.float32)
    upstream_all = upstream_all.reshape(N_CTX, T_DEV, H, HEAD).transpose(0, 2, 1, 3)

    def local_state(items):
        keys_part, value_part, ending_part = items
        key_feat = rounded(features(keys_part.astype(jnp.float32)))
        masked = key_feat * ending_part[None, :, None]
        state_part = jnp.einsum('htf,htd->hfd', masked, value_part.astype(jnp.float32), precision=highest)
        return (state_part, lax.optimization_barrier(jnp.sum(masked, axis=1)))
    state_local, norm_local = lax.map(local_state, (paired[:, :, 1], value_rows, ending))

    def forward_step(carry, items):
        state_part, norm_part, restart_part = items
        retained = 1.0 - restart_part
        return ((state_part + retained * carry[0], norm_part + retained * carry[1]), carry)
    zeros_state = (jnp.zeros((H, FEAT, HEAD), jnp.float32), jnp.zeros((H, FEAT), jnp.float32))
    unused, (state_in, norm_in) = lax.scan(forward_step, zeros_state, (state_local, norm_local, restart))

    def local_grads(items):
        queries, keys_all, value_part, upstream, segment_part, near_rows, state_part, norm_part = items
        places = jnp.arange(T_DEV, dtype=jnp.int32)
        query_float = queries.astype(jnp.float32)
        key_float = keys_all.astype(jnp.float32)
        value_float = value_part.astype(jnp.float32)
        query_feat = rounded(features(query_float))
        state_r = rounded(state_part)
        scores = jnp.einsum('hid,hjd->hij', query_float, key_float, precision=highest) * 0.25
        visible = (places[None, :] <= places[:, None]) & (segment_part[:, None] == segment_part[None, :])
        weight = jnp.where(visible[None], 1.0 + scores + 0.5 * scores * scores, 0.0)
        weight_r = rounded(weight)
        from_state = jnp.einsum('hif,hfd->hid', query_feat, state_r, precision=highest)
        numerator = jnp.einsum('hij,hjd->hid', weight_r, value_float, precision=highest) + near_rows[None, :, None] * from_state
        denominator = lax.optimization_barrier(jnp.sum(weight, axis=2)) + near_rows[None, :] * jnp.einsum('hif,hf->hi', query_feat, norm_part, precision=highest)
        attended = numerator / denominator[:, :, None]
        den_grad = -lax.optimization_barrier(jnp.sum(upstream * attended, axis=2)) / denominator
        num_float = rounded(upstream / denominator[:, :, None])
        mix_grad = jnp.einsum('hid,hjd->hij', num_float, value_float, precision=highest) + den_grad[:, :, None]
        score_grad = rounded(jnp.where(visible[None], mix_grad * (1.0 + scores), 0.0))
        value_grad = jnp.einsum('hij,hid->hjd', weight_r, num_float, precision=highest)
        key_grad = 0.25 * jnp.einsum('hij,hid->hjd', score_grad, query_float, precision=highest)
        feat_grad = near_rows[None, :, None] * (jnp.einsum('hid,hfd->hif', num_float, state_r, precision=highest) + den_grad[:, :, None] * norm_part[:, None, :])
        query_grad = 0.25 * jnp.einsum('hij,hjd->hid', score_grad, key_float, precision=highest) + feature_grad(feat_grad, query_float)
        near_feat = query_feat * near_rows[None, :, None]
        adj_part = jnp.einsum('hif,hid->hfd', near_feat, num_float, precision=highest)
        nadj_part = jnp.einsum('hif,hi->hf', near_feat, den_grad, precision=highest)
        return (attended.astype(jnp.bfloat16), query_grad.astype(jnp.bfloat16), key_grad, value_grad, adj_part, nadj_part)
    attended, query_grad, key_grad, value_grad, adj_local, nadj_local = lax.map(local_grads, (paired[:, :, 0], paired[:, :, 1], value_rows, upstream_all, segment, carried, state_in, norm_in))

    def backward_step(carry, items):
        adj_part, nadj_part, restart_part = items
        retained = 1.0 - restart_part
        return ((adj_part + retained * carry[0], nadj_part + retained * carry[1]), carry)
    unused, (adj_in, nadj_in) = lax.scan(backward_step, zeros_state, (adj_local, nadj_local, restart), reverse=True)

    def finish(items):
        keys_all, value_part, ending_part, key_part, value_part_grad, adj_part, nadj_part = items
        key_float = keys_all.astype(jnp.float32)
        key_feat = rounded(features(key_float))
        adj_r = rounded(adj_part)
        ending_col = ending_part[None, :, None]
        value_total = value_part_grad + ending_col * jnp.einsum('htf,hfd->htd', key_feat, adj_r, precision=highest)
        key_feat_grad = ending_col * (jnp.einsum('htd,hfd->htf', value_part.astype(jnp.float32), adj_r, precision=highest) + nadj_part[:, None, :])
        key_total = key_part + feature_grad(key_feat_grad, key_float)
        return (key_total.astype(jnp.bfloat16), value_total.astype(jnp.bfloat16))
    key_out, value_out = lax.map(finish, (paired[:, :, 1], value_rows, ending, key_grad, value_grad, adj_in, nadj_in))
    attended_flat = attended.transpose(0, 2, 1, 3).reshape(NTOK, H * HEAD)
    proj_grad = jnp.dot(attended_flat.T, out_grad, preferred_element_type=jnp.float32)
    qk_grad = jnp.stack([query_grad, key_out], axis=2).transpose(0, 3, 1, 2, 4).reshape(NTOK, H * 2 * QK)
    value_grad_out = value_out.transpose(0, 2, 1, 3).reshape(NTOK, H * HEAD)
    return (qk_grad, value_grad_out, proj_grad)
```

```python
import functools
import math

import jax
import jax.numpy as jnp
import numpy as np
from jax import lax
from jax.experimental import pallas as pl
from jax.experimental.pallas import tpu as pltpu
from jax.sharding import PartitionSpec as P

HEAD = 128
QK = 16
HEADS = 4
TOK = 512
FEAT = 160
QUAD = 0.25 / math.sqrt(2.0)
bf16 = jnp.bfloat16
f32 = jnp.float32
LIMIT = 56 * 1024 * 1024


def feature_tables():
    pairs = [(a, b) for a in range(QK) for b in range(a, QK)]
    pick = np.zeros((FEAT, 2 * QK), np.float32)
    cols = np.zeros((FEAT, HEAD), np.float32)
    cols[0, :4] = (1.0, 1.0, 1.0, 1.0)
    for a in range(QK):
        pick[1 + a, a] = 1.0
        cols[1 + a, :4] = (0.0, 1.0, 0.5, 1.0)
    for n, (a, b) in enumerate(pairs):
        row = 1 + QK + n
        pick[row, a] = 1.0
        pick[row, QK + b] = 1.0
        cols[row, :4] = (0.0, 0.0, QUAD, 1.0 if a == b else 2.0)
    return pick, pick.T.copy(), cols


def shift(k):
    return [(i, i + k) for i in range(32) if 0 <= i + k < 32]


def dot(a, b, ca, cb):
    return lax.dot_general(a, b, (((ca,), (cb,)), ((), ())), preferred_element_type=f32)


def call(body, outs, n_in, flops, nbytes, scalar=True):
    specs = [pl.BlockSpec(memory_space=pltpu.VMEM)] * n_in
    if scalar:
        specs = [pl.BlockSpec(memory_space=pltpu.SMEM)] + specs
    return pl.pallas_call(
        body,
        out_shape=[jax.ShapeDtypeStruct(s, t) for s, t in outs],
        in_specs=specs,
        out_specs=[pl.BlockSpec(memory_space=pltpu.VMEM)] * len(outs),
        compiler_params=pltpu.CompilerParams(vmem_limit_bytes=LIMIT),
        cost_estimate=pl.CostEstimate(flops=flops, bytes_accessed=nbytes, transcendentals=0),
    )


def lifted(pick, cols, x):
    a = dot(pick[:, :QK], x, 1, 0) + cols[:, 0:1]
    b = dot(pick[:, QK : 2 * QK], x, 1, 0) + cols[:, 1:2]
    return a, b, ((a * b) * cols[:, 2:3]).astype(bf16)


def split(x):
    high = x.astype(bf16)
    return high, (x - high.astype(f32)).astype(bf16)


def chain(pick_t, cols, g, a, b):
    scaled = g * cols[:, 2:3]
    out = jnp.zeros((QK, TOK), f32)
    for table, other in ((pick_t[:QK], b), (pick_t[QK : 2 * QK], a)):
        high, low = split(scaled * other)
        out = out + dot(table, high, 1, 0) + dot(table, low, 1, 0)
    return out


def put_norms(ref, norms):
    lane = lax.broadcasted_iota(jnp.int32, (FEAT, HEAD), 1)
    total = jnp.zeros((FEAT, HEAD), f32)
    for h in range(HEADS):
        high, low = split(norms[h])
        total = jnp.where(lane == h, high.astype(f32), total)
        total = jnp.where(lane == HEADS + h, low.astype(f32), total)
    ref[HEADS] = total.astype(bf16)


def norm_of(near, far, keep, h):
    def one(ref):
        part = ref[HEADS].astype(f32)
        return part[:, h : h + 1] + part[:, HEADS + h : HEADS + h + 1]

    return one(near) + keep * one(far)


def state_of(near, far, keep, h):
    return (near[h].astype(f32) + keep * far[h].astype(f32)).astype(bf16)


def local_state(ids, lens, qk, v, pick, cols, out, qkt, aux):
    off = ids[0].astype(f32)
    length = lens[...].astype(f32)
    later = lax.broadcasted_iota(jnp.int32, (128, 128), 1) < lax.broadcasted_iota(
        jnp.int32, (128, 128), 0
    )
    first = jnp.sum(jnp.where(later, length, 0.0), axis=1, keepdims=True) - off

    def doc_at(where_to):
        return jnp.max(jnp.where(first <= where_to, first, -1e9), axis=0, keepdims=True)

    start = doc_at(lax.broadcasted_iota(jnp.int32, (128, TOK), 1).astype(f32))
    last, prev, far = doc_at(TOK - 1.0), doc_at(-1.0), doc_at(3 * TOK - 1.0)
    ending = (start == last).astype(f32)
    aux[0:1] = start
    aux[1:2] = ending
    aux[2:3] = (start < 0.0).astype(f32)
    aux[3:4] = jnp.broadcast_to((last < 0.0).astype(f32), (1, TOK))
    aux[4:5] = jnp.broadcast_to((prev < -2.0 * TOK).astype(f32), (1, TOK))
    aux[5:6] = jnp.broadcast_to((far < 1.0 * TOK).astype(f32), (1, TOK))
    aux[6:8] = jnp.zeros((2, TOK), f32)
    qkt[...] = qk[...].astype(f32).T.astype(bf16)
    norms = []
    table, column = pick[...], cols[...]
    for h in range(HEADS):
        feat = lifted(table, column, qkt[32 * h + QK : 32 * h + 2 * QK])[2]
        feat = jnp.where(ending > 0.5, feat.astype(f32), 0.0)
        norms.append(jnp.sum(feat, axis=1, keepdims=True) * column[:, 3:4])
        state = dot(feat.astype(bf16), v[:, HEAD * h : HEAD * (h + 1)], 1, 0)
        out[h] = (state * column[:, 3:4]).astype(bf16)
    put_norms(out, norms)


def pair_sum(own, got, aux, out):
    keep = aux[3:4, 0:1]
    for h in range(HEADS):
        out[h] = (own[h].astype(f32) + keep * got[h].astype(f32)).astype(bf16)
    put_norms(out, [norm_of(own, got, keep, h) for h in range(HEADS)])


def scores_of(qkt, aux, h):
    q, k = qkt[32 * h : 32 * h + QK], qkt[32 * h + QK : 32 * h + 2 * QK]
    scores = dot(k, q, 0, 0) * 0.25
    row = lax.broadcasted_iota(jnp.int32, (TOK, TOK), 0)
    col = lax.broadcasted_iota(jnp.int32, (TOK, TOK), 1)
    visible = (row >= aux[0:1].astype(jnp.int32)) & (row <= col)
    return scores, visible, jnp.where(visible, 1.0 + scores + 0.5 * scores * scores, 0.0)


def attend(qkt, v, aux, pick, cols, near, far, att, quotient, dens):
    keep = aux[4:5, 0:1]
    carried = aux[2:3]
    table, column = pick[...], cols[...]
    for h in range(HEADS):
        rows = slice(HEAD * h, HEAD * (h + 1))
        weight = scores_of(qkt, aux, h)[2]
        feat = lifted(table, column, qkt[32 * h : 32 * h + QK])[2]
        norm = norm_of(near, far, keep, h)
        den = jnp.sum(weight, axis=0, keepdims=True)
        den = den + carried * jnp.sum(feat.astype(f32) * norm, axis=0, keepdims=True)
        num = dot(v[:, rows], weight.astype(bf16), 0, 0)
        num = num + carried * dot(state_of(near, far, keep, h), feat, 0, 0)
        y = num / den
        quotient[rows] = y
        att[rows] = y.astype(bf16)
        dens[h : h + 1] = den
    dens[HEADS:] = jnp.ones((8 - HEADS, TOK), f32)


def shard_of(ids, k):
    return lax.rem(ids[3] + k + 8, 8)


def partial_terms(count, ids, att, *refs):
    parts, (send, keep) = refs[: 2 * count], refs[2 * count :]
    first = ids[2] == 0
    half = TOK // 2
    for n in range(count):
        both = dot(att[:, :half], parts[2 * n][...], 1, 0)
        both = (both + dot(att[:, half:], parts[2 * n + 1][...], 1, 0)).astype(bf16)
        for j in range(2):
            even = both[:, 256 * j : 256 * j + HEAD]
            odd = both[:, 256 * j + HEAD : 256 * (j + 1)]
            send[2 * n + j] = jnp.where(first, odd, even)
            keep[2 * n + j] = jnp.where(first, even, odd)


def sum_cores(steps, ids, *refs):
    count = len(steps)
    out = refs[2 * count]
    for group, shards in enumerate(steps):
        for n, k in enumerate(shards):
            for j in range(2):
                total = refs[group][2 * n + j].astype(f32) + refs[count + group][2 * n + j].astype(f32)
                out[2 * shard_of(ids, k) + j] = total.astype(bf16)


def upstream(order, ids, w, *refs):
    parts, up = refs[:-1], refs[-1]
    half = TOK // 2
    for p in range(2):
        total = jnp.zeros((TOK, half), f32)
        for n, k in enumerate(order):
            at = pl.multiple_of(shard_of(ids, k) * TOK, TOK)
            total = total + dot(w[:, pl.ds(at, TOK)], parts[2 * n + p][...], 1, 1)
        up[:, half * p : half * (p + 1)] = total


def local_adjoint(up, quotient, dens, qkt, aux, pick, cols, ng, dg, out):
    carried = aux[2:3]
    table, column = pick[...], cols[...]
    norms = []
    for h in range(HEADS):
        rows = slice(HEAD * h, HEAD * (h + 1))
        inv = 1.0 / dens[h : h + 1]
        upstream = up[rows]
        den_grad = -jnp.sum(upstream * quotient[rows], axis=0, keepdims=True) * inv
        num_grad = (upstream * inv).astype(bf16)
        ng[rows] = num_grad
        dg[h : h + 1] = den_grad
        feat = lifted(table, column, qkt[32 * h : 32 * h + QK])[2]
        feat = feat.astype(f32) * carried
        norms.append(jnp.sum(feat * den_grad, axis=1, keepdims=True) * column[:, 3:4])
        out[h] = (dot(feat.astype(bf16), num_grad, 1, 1) * column[:, 3:4]).astype(bf16)
    dg[HEADS:] = jnp.zeros((8 - HEADS, TOK), f32)
    put_norms(out, norms)


def local_grads(ng, dg, qkt, v, aux, pick, pick_t, cols, near, far, qkg, vg):
    keep = aux[4:5, 0:1]
    carried = aux[2:3]
    table, column = pick[...], cols[...]
    for h in range(HEADS):
        rows = slice(HEAD * h, HEAD * (h + 1))
        q, k = qkt[32 * h : 32 * h + QK], qkt[32 * h + QK : 32 * h + 2 * QK]
        scores, visible, weight = scores_of(qkt, aux, h)
        num_grad, den_grad = ng[rows], dg[h : h + 1]
        mix = dot(v[:, rows], num_grad, 1, 0) + den_grad
        score_grad = jnp.where(visible, mix * (1.0 + scores), 0.0).astype(bf16)
        vg[:, rows] = dot(weight.astype(bf16), num_grad, 1, 1)
        a, b, _ = lifted(table, column, q)
        g = dot(state_of(near, far, keep, h), num_grad, 1, 0)
        g = carried * (g + norm_of(near, far, keep, h) * den_grad)
        qkg[32 * h : 32 * h + QK] = 0.25 * dot(k, score_grad, 1, 0) + chain(
            pick_t[...], column, g, a, b
        )
        qkg[32 * h + QK : 32 * h + 2 * QK] = 0.25 * dot(q, score_grad, 1, 1)


def finish(qkg, vg, qkt, v, aux, pick, pick_t, cols, near, far, qk_out, v_out, acc):
    keep = aux[5:6, 0:1]
    ending = aux[1:2]
    table, column = pick[...], cols[...]
    for h in range(HEADS):
        rows = slice(HEAD * h, HEAD * (h + 1))
        a, b, feat = lifted(table, column, qkt[32 * h + QK : 32 * h + 2 * QK])
        feat = (feat.astype(f32) * ending).astype(bf16)
        adjoint = state_of(near, far, keep, h)
        v_out[:, rows] = (vg[:, rows] + dot(feat, adjoint, 0, 0)).astype(bf16)
        g = dot(adjoint, v[:, rows], 1, 1) + norm_of(near, far, keep, h)
        acc[32 * h : 32 * h + QK] = qkg[32 * h : 32 * h + QK]
        acc[32 * h + QK : 32 * h + 2 * QK] = qkg[32 * h + QK : 32 * h + 2 * QK] + chain(
            pick_t[...], column, g * ending, a, b
        )
    qk_out[...] = acc[...].T.astype(bf16)


def on_device(query_key, values, out_grad, out_weight, doc_lengths):
    c = lax.axis_index("ctx").astype(jnp.int32)
    ids = jnp.stack([c * TOK, c // 2, c % 2, lax.axis_index("head").astype(jnp.int32)])
    np_pick, np_pick_t, np_cols = feature_tables()
    pick, pick_t, cols = jnp.asarray(np_pick, bf16), jnp.asarray(np_pick_t, bf16), jnp.asarray(np_cols)
    slab = ((HEADS + 1, FEAT, HEAD), bf16)

    half = TOK // 2
    own = [out_grad[:half], out_grad[half:]]
    pieces = {0: own}
    ring = {d: [(i, (i + d) % 8) for i in range(8)] for d in (1, -1)}
    for step in range(1, 4):
        for d in (1, -1):
            before = pieces[-d * (step - 1)]
            pieces[-d * step] = [lax.ppermute(x, "head", ring[d]) for x in before]
    pieces[4] = [lax.ppermute(pieces[-3][0], "head", ring[1]), lax.ppermute(pieces[3][1], "head", ring[-1])]

    local, qkt, aux = call(
        local_state,
        [slab, ((128, TOK), bf16), ((8, TOK), f32)],
        5,
        2**27,
        2**21,
    )(ids, doc_lengths.reshape(1, 128), query_key, values, pick, cols)

    def exchange(mine, sign):
        got = lax.ppermute(mine, "ctx", shift(sign))
        pair = call(pair_sum, [slab], 3, 2**20, 2**20, False)(mine, got, aux)[0]
        return lax.ppermute(pair, "ctx", shift(sign)), lax.ppermute(pair, "ctx", shift(3 * sign))

    near, far = exchange(local, 1)
    att, quotient, dens = call(
        attend,
        [((TOK, TOK), bf16), ((TOK, TOK), f32), ((8, TOK), f32)],
        7,
        2**30,
        4 * 2**20,
        False,
    )(qkt, values, aux, pick, cols, near, far)

    steps = [(0, -1, 1), (-2, 2), (-3, 3), (4,)]
    keeps, gots = [], []
    for shards in steps:
        n = len(shards)
        block = ((2 * n, TOK, HEAD), bf16)
        send, keep = call(
            functools.partial(partial_terms, n), [block, block], 1 + 2 * n, n * 2**28, 2**20 * n
        )(ids, att, *[x for k in shards for x in pieces[k]])
        keeps.append(keep)
        gots.append(lax.ppermute(send, "ctx", [(i, i ^ 1) for i in range(32)]))
    summed = call(
        functools.partial(sum_cores, steps), [((16, TOK, HEAD), bf16)], 8, 2**21, 6 * 2**20
    )(ids, *keeps, *gots)[0]
    chips = [[2 * j + k for j in range(16)] for k in range(2)]
    spread = lax.all_to_all(summed, "ctx", 0, 0, axis_index_groups=chips)
    proj_grad = jnp.sum(spread.astype(f32), axis=0)

    order = [k for shards in steps for k in shards]
    up = call(functools.partial(upstream, order), [((TOK, TOK), f32)], 17, 2**32, 9 * 2**20)(
        ids, out_weight, *[x for k in order for x in pieces[k]]
    )[0]

    ng, dg, adj_local = call(
        local_adjoint,
        [((TOK, TOK), bf16), ((8, TOK), f32), slab],
        7,
        2**28,
        4 * 2**20,
        False,
    )(up, quotient, dens, qkt, aux, pick, cols)
    adj_near, adj_far = exchange(adj_local, -1)
    qkg, vg = call(
        local_grads, [((128, TOK), f32), ((TOK, TOK), f32)], 10, 2**31, 4 * 2**20, False
    )(ng, dg, qkt, values, aux, pick, pick_t, cols, near, far)
    qk_grad, value_grad = pl.pallas_call(
        finish,
        out_shape=[
            jax.ShapeDtypeStruct((TOK, 128), bf16),
            jax.ShapeDtypeStruct((TOK, TOK), bf16),
        ],
        in_specs=[pl.BlockSpec(memory_space=pltpu.VMEM)] * 10,
        out_specs=[pl.BlockSpec(memory_space=pltpu.VMEM)] * 2,
        scratch_shapes=[pltpu.VMEM((128, TOK), f32)],
        compiler_params=pltpu.CompilerParams(vmem_limit_bytes=LIMIT),
        cost_estimate=pl.CostEstimate(flops=2**29, bytes_accessed=4 * 2**20, transcendentals=0),
    )(qkg, vg, qkt, values, aux, pick, pick_t, cols, adj_near, adj_far)
    return (qk_grad, value_grad, proj_grad)


def solution(mesh):
    placed = (P("ctx", "head"), P("ctx", "head"), P("ctx", "head"), P("head", None), P())
    return jax.shard_map(
        on_device,
        mesh=mesh,
        in_specs=placed,
        out_specs=(P("ctx", "head"), P("ctx", "head"), P("head", "ctx")),
        check_vma=False,
    )
```

```python
import functools
import math

import jax
import jax.numpy as jnp
import numpy as np
from jax import lax
from jax.experimental import pallas as pl
from jax.experimental.pallas import tpu as pltpu
from jax.sharding import PartitionSpec as P

HEAD = 128
QK = 16
HEADS = 4
TOK = 512
FEAT = 160
QUAD = 0.25 / math.sqrt(2.0)
bf16 = jnp.bfloat16
f32 = jnp.float32
LIMIT = 20 * 1024 * 1024


def feature_tables():
    pairs = [(a, b) for a in range(QK) for b in range(a, QK)]
    pick = np.zeros((FEAT, 2 * QK), np.float32)
    cols = np.zeros((FEAT, HEAD), np.float32)
    cols[0, :4] = (1.0, 1.0, 1.0, 1.0)
    for a in range(QK):
        pick[1 + a, a] = 1.0
        cols[1 + a, :4] = (0.0, 1.0, 0.5, 1.0)
    for n, (a, b) in enumerate(pairs):
        row = 1 + QK + n
        pick[row, a] = 1.0
        pick[row, QK + b] = 1.0
        cols[row, :4] = (0.0, 0.0, QUAD, 1.0 if a == b else 2.0)
    return pick, pick.T.copy(), cols


def place(i):
    return i // 8, (i // 2) % 4, i % 2


def index(y, x, k):
    return ((y % 4) * 4 + x % 4) * 2 + k


def along(dy, dx):
    return [(i, index(place(i)[0] + dy, place(i)[1] + dx, i % 2)) for i in range(32)]


def shift(k):
    return [(i, i + k) for i in range(32) if 0 <= i + k < 32]


def dot(a, b, ca, cb):
    return lax.dot_general(a, b, (((ca,), (cb,)), ((), ())), preferred_element_type=f32)


def call(body, outs, n_in, flops, nbytes, scalar=True):
    specs = [pl.BlockSpec(memory_space=pltpu.VMEM)] * n_in
    if scalar:
        specs = [pl.BlockSpec(memory_space=pltpu.SMEM)] + specs
    return pl.pallas_call(
        body,
        out_shape=[jax.ShapeDtypeStruct(s, t) for s, t in outs],
        in_specs=specs,
        out_specs=[pl.BlockSpec(memory_space=pltpu.VMEM)] * len(outs),
        compiler_params=pltpu.CompilerParams(vmem_limit_bytes=LIMIT),
        cost_estimate=pl.CostEstimate(flops=flops, bytes_accessed=nbytes, transcendentals=0),
    )


def lifted(pick, cols, x):
    a = dot(pick[:, :QK], x, 1, 0) + cols[:, 0:1]
    b = dot(pick[:, QK : 2 * QK], x, 1, 0) + cols[:, 1:2]
    return a, b, ((a * b) * cols[:, 2:3]).astype(bf16)


def split(x):
    high = x.astype(bf16)
    return high, (x - high.astype(f32)).astype(bf16)


def chain(pick_t, cols, g, a, b):
    scaled = g * cols[:, 2:3]
    out = jnp.zeros((QK, TOK), f32)
    for table, other in ((pick_t[:QK], b), (pick_t[QK : 2 * QK], a)):
        high, low = split(scaled * other)
        out = out + dot(table, high, 1, 0) + dot(table, low, 1, 0)
    return out


def put_norms(ref, norms):
    lane = lax.broadcasted_iota(jnp.int32, (FEAT, HEAD), 1)
    total = jnp.zeros((FEAT, HEAD), f32)
    for h in range(HEADS):
        high, low = split(norms[h])
        total = jnp.where(lane == h, high.astype(f32), total)
        total = jnp.where(lane == HEADS + h, low.astype(f32), total)
    ref[HEADS] = total.astype(bf16)


def norm_of(near, far, keep, h):
    def one(ref):
        part = ref[HEADS].astype(f32)
        return part[:, h : h + 1] + part[:, HEADS + h : HEADS + h + 1]

    return one(near) + keep * one(far)


def state_of(near, far, keep, h):
    return (near[h].astype(f32) + keep * far[h].astype(f32)).astype(bf16)


def local_state(ids, lens, qk, v, pick, cols, out, qkt, aux):
    off = ids[0].astype(f32)
    length = lens[...].astype(f32)
    later = lax.broadcasted_iota(jnp.int32, (128, 128), 1) < lax.broadcasted_iota(
        jnp.int32, (128, 128), 0
    )
    first = jnp.sum(jnp.where(later, length, 0.0), axis=1, keepdims=True) - off

    def doc_at(where_to):
        return jnp.max(jnp.where(first <= where_to, first, -1e9), axis=0, keepdims=True)

    start = doc_at(lax.broadcasted_iota(jnp.int32, (128, TOK), 1).astype(f32))
    last, prev, far = doc_at(TOK - 1.0), doc_at(-1.0), doc_at(3 * TOK - 1.0)
    ending = (start == last).astype(f32)
    aux[0:1] = start
    aux[1:2] = ending
    aux[2:3] = (start < 0.0).astype(f32)
    aux[3:4] = jnp.broadcast_to((last < 0.0).astype(f32), (1, TOK))
    aux[4:5] = jnp.broadcast_to((prev < -2.0 * TOK).astype(f32), (1, TOK))
    aux[5:6] = jnp.broadcast_to((far < 1.0 * TOK).astype(f32), (1, TOK))
    aux[6:8] = jnp.zeros((2, TOK), f32)
    qkt[...] = qk[...].astype(f32).T.astype(bf16)
    norms = []
    table, column = pick[...], cols[...]
    for h in range(HEADS):
        feat = lifted(table, column, qkt[32 * h + QK : 32 * h + 2 * QK])[2]
        feat = jnp.where(ending > 0.5, feat.astype(f32), 0.0)
        norms.append(jnp.sum(feat, axis=1, keepdims=True) * column[:, 3:4])
        state = dot(feat.astype(bf16), v[:, HEAD * h : HEAD * (h + 1)], 1, 0)
        out[h] = (state * column[:, 3:4]).astype(bf16)
    put_norms(out, norms)


def pair_sum(own, got, aux, out):
    keep = aux[3:4, 0:1]
    for h in range(HEADS):
        out[h] = (own[h].astype(f32) + keep * got[h].astype(f32)).astype(bf16)
    put_norms(out, [norm_of(own, got, keep, h) for h in range(HEADS)])


def scores_of(qkt, aux, h):
    q, k = qkt[32 * h : 32 * h + QK], qkt[32 * h + QK : 32 * h + 2 * QK]
    scores = dot(k, q, 0, 0) * 0.25
    row = lax.broadcasted_iota(jnp.int32, (TOK, TOK), 0)
    col = lax.broadcasted_iota(jnp.int32, (TOK, TOK), 1)
    visible = (row >= aux[0:1].astype(jnp.int32)) & (row <= col)
    return scores, visible, jnp.where(visible, 1.0 + scores + 0.5 * scores * scores, 0.0)


def attend(qkt, v, aux, pick, cols, near, far, att, quotient, dens):
    keep = aux[4:5, 0:1]
    carried = aux[2:3]
    table, column = pick[...], cols[...]
    for h in range(HEADS):
        rows = slice(HEAD * h, HEAD * (h + 1))
        weight = scores_of(qkt, aux, h)[2]
        feat = lifted(table, column, qkt[32 * h : 32 * h + QK])[2]
        norm = norm_of(near, far, keep, h)
        den = jnp.sum(weight, axis=0, keepdims=True)
        den = den + carried * jnp.sum(feat.astype(f32) * norm, axis=0, keepdims=True)
        num = dot(v[:, rows], weight.astype(bf16), 0, 0)
        num = num + carried * dot(state_of(near, far, keep, h), feat, 0, 0)
        y = num / den
        quotient[rows] = y
        att[rows] = y.astype(bf16)
        dens[h : h + 1] = den
    dens[HEADS:] = jnp.ones((8 - HEADS, TOK), f32)


def shard_of(ids, k):
    return lax.rem(ids[3] + k + 8, 8)


def partial_terms(count, ids, att, *refs):
    parts, (send, keep) = refs[: 2 * count], refs[2 * count :]
    first = ids[2] == 0
    half = TOK // 2
    for n in range(count):
        both = dot(att[:, :half], parts[2 * n][...], 1, 0)
        both = (both + dot(att[:, half:], parts[2 * n + 1][...], 1, 0)).astype(bf16)
        for j in range(2):
            even = both[:, 256 * j : 256 * j + HEAD]
            odd = both[:, 256 * j + HEAD : 256 * (j + 1)]
            send[2 * n + j] = jnp.where(first, odd, even)
            keep[2 * n + j] = jnp.where(first, even, odd)


def sum_cores(steps, ids, *refs):
    count = len(steps)
    outs, whole = refs[2 * count : -1], refs[-1]
    half = TOK // 2
    for group, shards in enumerate(steps):
        for n, k in enumerate(shards):
            for j in range(2):
                total = refs[group][2 * n + j].astype(f32) + refs[count + group][2 * n + j].astype(f32)
                whole[2 * shard_of(ids, k) + j] = total.astype(bf16)
    for d in range(4):
        x, y = lax.rem(ids[5] + d, 4), lax.rem(ids[4] + d, 4)
        for n in range(4):
            outs[d][n] = whole[4 * n + x, :half]
            outs[4 + d][n] = whole[4 * y + n, half:]


def add_up(refs, *at):
    total = refs[0][at].astype(f32)
    for ref in refs[1:]:
        total = total + ref[at].astype(f32)
    return total


def sum_first(ids, *refs):
    ins, outs = refs[:8], refs[8:]
    for side in range(2):
        for d in range(4):
            at = lax.rem(ids[4 + side] + d, 4)
            out = outs[4 * side + d]
            out[...] = add_up(ins[4 * side : 4 * side + 4], at).astype(out.dtype)


def sum_last(*refs):
    half = TOK // 2
    for side in range(2):
        refs[8][half * side : half * (side + 1)] = add_up(refs[4 * side : 4 * side + 4], Ellipsis)


def upstream(order, ids, w, *refs):
    parts, up = refs[:-1], refs[-1]
    half = TOK // 2
    for p in range(2):
        total = jnp.zeros((TOK, half), f32)
        for n, k in enumerate(order):
            at = pl.multiple_of(shard_of(ids, k) * TOK, TOK)
            total = total + dot(w[:, pl.ds(at, TOK)], parts[2 * n + p][...], 1, 1)
        up[:, half * p : half * (p + 1)] = total


def local_adjoint(up, quotient, dens, qkt, aux, pick, cols, ng, dg, out):
    carried = aux[2:3]
    table, column = pick[...], cols[...]
    norms = []
    for h in range(HEADS):
        rows = slice(HEAD * h, HEAD * (h + 1))
        inv = 1.0 / dens[h : h + 1]
        upstream = up[rows]
        den_grad = -jnp.sum(upstream * quotient[rows], axis=0, keepdims=True) * inv
        num_grad = (upstream * inv).astype(bf16)
        ng[rows] = num_grad
        dg[h : h + 1] = den_grad
        feat = lifted(table, column, qkt[32 * h : 32 * h + QK])[2]
        feat = feat.astype(f32) * carried
        norms.append(jnp.sum(feat * den_grad, axis=1, keepdims=True) * column[:, 3:4])
        out[h] = (dot(feat.astype(bf16), num_grad, 1, 1) * column[:, 3:4]).astype(bf16)
    dg[HEADS:] = jnp.zeros((8 - HEADS, TOK), f32)
    put_norms(out, norms)


def local_grads(ng, dg, qkt, v, aux, pick, pick_t, cols, near, far, qkg, vg):
    keep = aux[4:5, 0:1]
    carried = aux[2:3]
    table, column = pick[...], cols[...]
    for h in range(HEADS):
        rows = slice(HEAD * h, HEAD * (h + 1))
        q, k = qkt[32 * h : 32 * h + QK], qkt[32 * h + QK : 32 * h + 2 * QK]
        scores, visible, weight = scores_of(qkt, aux, h)
        num_grad, den_grad = ng[rows], dg[h : h + 1]
        mix = dot(v[:, rows], num_grad, 1, 0) + den_grad
        score_grad = jnp.where(visible, mix * (1.0 + scores), 0.0).astype(bf16)
        vg[:, rows] = dot(weight.astype(bf16), num_grad, 1, 1)
        a, b, _ = lifted(table, column, q)
        g = dot(state_of(near, far, keep, h), num_grad, 1, 0)
        g = carried * (g + norm_of(near, far, keep, h) * den_grad)
        qkg[32 * h : 32 * h + QK] = 0.25 * dot(k, score_grad, 1, 0) + chain(
            pick_t[...], column, g, a, b
        )
        qkg[32 * h + QK : 32 * h + 2 * QK] = 0.25 * dot(q, score_grad, 1, 1)


def finish(qkg, vg, qkt, v, aux, pick, pick_t, cols, near, far, qk_out, v_out, acc):
    keep = aux[5:6, 0:1]
    ending = aux[1:2]
    table, column = pick[...], cols[...]
    for h in range(HEADS):
        rows = slice(HEAD * h, HEAD * (h + 1))
        a, b, feat = lifted(table, column, qkt[32 * h + QK : 32 * h + 2 * QK])
        feat = (feat.astype(f32) * ending).astype(bf16)
        adjoint = state_of(near, far, keep, h)
        v_out[:, rows] = (vg[:, rows] + dot(feat, adjoint, 0, 0)).astype(bf16)
        g = dot(adjoint, v[:, rows], 1, 1) + norm_of(near, far, keep, h)
        acc[32 * h : 32 * h + QK] = qkg[32 * h : 32 * h + QK]
        acc[32 * h + QK : 32 * h + 2 * QK] = qkg[32 * h + QK : 32 * h + 2 * QK] + chain(
            pick_t[...], column, g * ending, a, b
        )
    qk_out[...] = acc[...].T.astype(bf16)


def on_device(query_key, values, out_grad, out_weight, doc_lengths):
    c = lax.axis_index("ctx").astype(jnp.int32)
    ids = jnp.stack([c * TOK, c // 2, c % 2, lax.axis_index("head").astype(jnp.int32), c // 8, (c // 2) % 4])
    np_pick, np_pick_t, np_cols = feature_tables()
    pick, pick_t, cols = jnp.asarray(np_pick, bf16), jnp.asarray(np_pick_t, bf16), jnp.asarray(np_cols)
    slab = ((HEADS + 1, FEAT, HEAD), bf16)

    half = TOK // 2
    own = lax.optimization_barrier([out_grad[:half], out_grad[half:]])
    query_key, own[0] = lax.optimization_barrier((query_key, own[0]))

    local, qkt, aux = call(
        local_state,
        [slab, ((128, TOK), bf16), ((8, TOK), f32)],
        5,
        2**27,
        2**21,
    )(ids, doc_lengths.reshape(1, 128), query_key, values, pick, cols)

    later, aux = lax.optimization_barrier((own[1], aux))
    own = [own[0], later]
    pieces = {0: own}
    ring = {d: [(i, (i + d) % 8) for i in range(8)] for d in (1, -1)}
    for step in range(1, 4):
        for d in (1, -1):
            before = pieces[-d * (step - 1)]
            pieces[-d * step] = [lax.ppermute(x, "head", ring[d]) for x in before]
    pieces[4] = [lax.ppermute(pieces[-3][0], "head", ring[1]), lax.ppermute(pieces[3][1], "head", ring[-1])]

    def exchange(mine, sign):
        got = lax.ppermute(mine, "ctx", shift(sign))
        pair = call(pair_sum, [slab], 3, 2**20, 2**20, False)(mine, got, aux)[0]
        return lax.ppermute(pair, "ctx", shift(sign)), lax.ppermute(pair, "ctx", shift(3 * sign))

    near, far = exchange(local, 1)
    att, quotient, dens = call(
        attend,
        [((TOK, TOK), bf16), ((TOK, TOK), f32), ((8, TOK), f32)],
        7,
        2**30,
        4 * 2**20,
        False,
    )(qkt, values, aux, pick, cols, near, far)

    steps = [(0, -1, 1), (-2, 2), (-3, 3), (4,)]
    keeps, gots = [], []
    for shards in steps:
        n = len(shards)
        block = ((2 * n, TOK, HEAD), bf16)
        send, keep = call(
            functools.partial(partial_terms, n), [block, block], 1 + 2 * n, n * 2**28, 2**20 * n
        )(ids, att, *[x for k in shards for x in pieces[k]])
        keeps.append(keep)
        gots.append(lax.ppermute(send, "ctx", [(i, i ^ 1) for i in range(32)]))
    order = [k for shards in steps for k in shards]
    up = call(functools.partial(upstream, order), [((TOK, TOK), f32)], 17, 2**32, 9 * 2**20)(
        ids, out_weight, *[x for k in order for x in pieces[k]]
    )[0]

    ng, dg, adj_local = call(
        local_adjoint,
        [((TOK, TOK), bf16), ((8, TOK), f32), slab],
        7,
        2**28,
        4 * 2**20,
        False,
    )(up, quotient, dens, qkt, aux, pick, cols)
    adj_near, adj_far = exchange(adj_local, -1)
    send = lambda x, pairs: lax.ppermute(x, "ctx", pairs)
    keeps[0], adj_local = lax.optimization_barrier((keeps[0], adj_local))
    parts = pl.pallas_call(
        functools.partial(sum_cores, steps),
        out_shape=[jax.ShapeDtypeStruct((4, half, HEAD), bf16)] * 8,
        in_specs=[pl.BlockSpec(memory_space=pltpu.SMEM)]
        + [pl.BlockSpec(memory_space=pltpu.VMEM)] * 8,
        out_specs=[pl.BlockSpec(memory_space=pltpu.VMEM)] * 8,
        scratch_shapes=[pltpu.VMEM((16, TOK, HEAD), bf16)],
        compiler_params=pltpu.CompilerParams(vmem_limit_bytes=LIMIT),
        cost_estimate=pl.CostEstimate(flops=2**21, bytes_accessed=6 * 2**20, transcendentals=0),
    )(ids, *keeps, *gots)
    gx = [send(parts[d], along(0, d)) for d in (1, 3, 2)]
    gy = [send(parts[4 + d], along(d, 0)) for d in (1, 3, 2)]
    qkg, vg = call(
        local_grads, [((128, TOK), f32), ((TOK, TOK), f32)], 10, 2**31, 4 * 2**20, False
    )(ng, dg, qkt, values, aux, pick, pick_t, cols, near, far)
    low, vg = lax.optimization_barrier((parts[0], vg))
    shapes = [((half, HEAD), f32 if n % 4 == 0 else bf16) for n in range(8)]
    sums = call(sum_first, shapes, 8, 2**21, 3 * 2**20)(ids, low, *gx, parts[4], *gy)
    gy = [send(sums[d], along(d, 0)) for d in (1, 3, 2)]
    gx = [send(sums[4 + d], along(0, d)) for d in (1, 3, 2)]
    proj_grad = call(sum_last, [((TOK, HEAD), f32)], 8, 2**19, 2**20, False)(
        sums[0], *gy, sums[4], *gx
    )[0]

    qk_grad, value_grad = pl.pallas_call(
        finish,
        out_shape=[
            jax.ShapeDtypeStruct((TOK, 128), bf16),
            jax.ShapeDtypeStruct((TOK, TOK), bf16),
        ],
        in_specs=[pl.BlockSpec(memory_space=pltpu.VMEM)] * 10,
        out_specs=[pl.BlockSpec(memory_space=pltpu.VMEM)] * 2,
        scratch_shapes=[pltpu.VMEM((128, TOK), f32)],
        compiler_params=pltpu.CompilerParams(vmem_limit_bytes=LIMIT),
        cost_estimate=pl.CostEstimate(flops=2**29, bytes_accessed=4 * 2**20, transcendentals=0),
    )(qkg, vg, qkt, values, aux, pick, pick_t, cols, adj_near, adj_far)
    return (qk_grad, value_grad, proj_grad)


def solution(mesh):
    placed = (P("ctx", "head"), P("ctx", "head"), P("ctx", "head"), P("head", None), P())
    return jax.shard_map(
        on_device,
        mesh=mesh,
        in_specs=placed,
        out_specs=(P("ctx", "head"), P("ctx", "head"), P("head", "ctx")),
        check_vma=False,
    )
```

```python
import functools
import math

import jax
import jax.numpy as jnp
import numpy as np
from jax import lax
from jax.experimental import pallas as pl
from jax.experimental.pallas import tpu as pltpu
from jax.sharding import PartitionSpec as P

HEAD = 128
QK = 16
HEADS = 4
TOK = 512
FEAT = 160
QUAD = 0.25 / math.sqrt(2.0)
bf16 = jnp.bfloat16
f32 = jnp.float32
MIB = 1024 * 1024
LIMIT = 20 * MIB


def feature_tables():
    pairs = [(a, b) for a in range(QK) for b in range(a, QK)]
    pick = np.zeros((FEAT, 2 * QK), np.float32)
    cols = np.zeros((FEAT, HEAD), np.float32)
    cols[0, :4] = (1.0, 1.0, 1.0, 1.0)
    for a in range(QK):
        pick[1 + a, a] = 1.0
        cols[1 + a, :4] = (0.0, 1.0, 0.5, 1.0)
    for n, (a, b) in enumerate(pairs):
        row = 1 + QK + n
        pick[row, a] = 1.0
        pick[row, QK + b] = 1.0
        cols[row, :4] = (0.0, 0.0, QUAD, 1.0 if a == b else 2.0)
    return pick, pick.T.copy(), cols


def place(i):
    return i // 8, (i // 2) % 4, i % 2


def index(y, x, k):
    return ((y % 4) * 4 + x % 4) * 2 + k


def along(dy, dx):
    return [(i, index(place(i)[0] + dy, place(i)[1] + dx, i % 2)) for i in range(32)]


def shift(k):
    return [(i, i + k) for i in range(32) if 0 <= i + k < 32]


def dot(a, b, ca, cb):
    return lax.dot_general(a, b, (((ca,), (cb,)), ((), ())), preferred_element_type=f32)


def call(body, outs, n_in, flops, nbytes, scalar=True, limit=LIMIT):
    specs = [pl.BlockSpec(memory_space=pltpu.VMEM)] * n_in
    if scalar:
        specs = [pl.BlockSpec(memory_space=pltpu.SMEM)] + specs
    return pl.pallas_call(
        body,
        out_shape=[jax.ShapeDtypeStruct(s, t) for s, t in outs],
        in_specs=specs,
        out_specs=[pl.BlockSpec(memory_space=pltpu.VMEM)] * len(outs),
        compiler_params=pltpu.CompilerParams(vmem_limit_bytes=limit),
        cost_estimate=pl.CostEstimate(flops=flops, bytes_accessed=nbytes, transcendentals=0),
    )


def lifted(pick, cols, x):
    a = dot(pick[:, :QK], x, 1, 0) + cols[:, 0:1]
    b = dot(pick[:, QK : 2 * QK], x, 1, 0) + cols[:, 1:2]
    return a, b, ((a * b) * cols[:, 2:3]).astype(bf16)


def split(x):
    high = x.astype(bf16)
    return high, (x - high.astype(f32)).astype(bf16)


def chain(pick_t, cols, g, a, b):
    scaled = g * cols[:, 2:3]
    out = jnp.zeros((QK, TOK), f32)
    for table, other in ((pick_t[:QK], b), (pick_t[QK : 2 * QK], a)):
        high, low = split(scaled * other)
        out = out + dot(table, high, 1, 0) + dot(table, low, 1, 0)
    return out


def put_norms(ref, norms):
    lane = lax.broadcasted_iota(jnp.int32, (FEAT, HEAD), 1)
    total = jnp.zeros((FEAT, HEAD), f32)
    for h in range(HEADS):
        high, low = split(norms[h])
        total = jnp.where(lane == h, high.astype(f32), total)
        total = jnp.where(lane == HEADS + h, low.astype(f32), total)
    ref[HEADS] = total.astype(bf16)


def norm_of(near, far, keep, h):
    def one(ref):
        part = ref[HEADS].astype(f32)
        return part[:, h : h + 1] + part[:, HEADS + h : HEADS + h + 1]

    return one(near) + keep * one(far)


def state_of(near, far, keep, h):
    return (near[h].astype(f32) + keep * far[h].astype(f32)).astype(bf16)


def local_state(ids, lens, qk, v, pick, cols, out, qkt, aux):
    off = ids[0].astype(f32)
    length = lens[...].astype(f32)
    later = lax.broadcasted_iota(jnp.int32, (128, 128), 1) < lax.broadcasted_iota(
        jnp.int32, (128, 128), 0
    )
    first = jnp.sum(jnp.where(later, length, 0.0), axis=1, keepdims=True) - off

    def doc_at(where_to):
        return jnp.max(jnp.where(first <= where_to, first, -1e9), axis=0, keepdims=True)

    start = doc_at(lax.broadcasted_iota(jnp.int32, (128, TOK), 1).astype(f32))
    last, prev, far = doc_at(TOK - 1.0), doc_at(-1.0), doc_at(3 * TOK - 1.0)
    ending = (start == last).astype(f32)
    aux[0:1] = start
    aux[1:2] = ending
    aux[2:3] = (start < 0.0).astype(f32)
    aux[3:4] = jnp.broadcast_to((last < 0.0).astype(f32), (1, TOK))
    aux[4:5] = jnp.broadcast_to((prev < -2.0 * TOK).astype(f32), (1, TOK))
    aux[5:6] = jnp.broadcast_to((far < 1.0 * TOK).astype(f32), (1, TOK))
    aux[6:8] = jnp.zeros((2, TOK), f32)
    qkt[...] = qk[...].astype(f32).T.astype(bf16)
    norms = []
    table, column = pick[...], cols[...]
    for h in range(HEADS):
        feat = lifted(table, column, qkt[32 * h + QK : 32 * h + 2 * QK])[2]
        feat = jnp.where(ending > 0.5, feat.astype(f32), 0.0)
        norms.append(jnp.sum(feat, axis=1, keepdims=True) * column[:, 3:4])
        state = dot(feat.astype(bf16), v[:, HEAD * h : HEAD * (h + 1)], 1, 0)
        out[h] = (state * column[:, 3:4]).astype(bf16)
    put_norms(out, norms)


def pair_sum(own, got, aux, out):
    keep = aux[3:4, 0:1]
    for h in range(HEADS):
        out[h] = (own[h].astype(f32) + keep * got[h].astype(f32)).astype(bf16)
    put_norms(out, [norm_of(own, got, keep, h) for h in range(HEADS)])


def scores_of(qkt, aux, h):
    q, k = qkt[32 * h : 32 * h + QK], qkt[32 * h + QK : 32 * h + 2 * QK]
    scores = dot(k, q, 0, 0) * 0.25
    row = lax.broadcasted_iota(jnp.int32, (TOK, TOK), 0)
    col = lax.broadcasted_iota(jnp.int32, (TOK, TOK), 1)
    visible = (row >= aux[0:1].astype(jnp.int32)) & (row <= col)
    return scores, visible, jnp.where(visible, 1.0 + scores + 0.5 * scores * scores, 0.0)


def attend(qkt, v, aux, pick, cols, near, far, att, quotient, dens):
    keep = aux[4:5, 0:1]
    carried = aux[2:3]
    table, column = pick[...], cols[...]
    for h in range(HEADS):
        rows = slice(HEAD * h, HEAD * (h + 1))
        weight = scores_of(qkt, aux, h)[2]
        feat = lifted(table, column, qkt[32 * h : 32 * h + QK])[2]
        norm = norm_of(near, far, keep, h)
        den = jnp.sum(weight, axis=0, keepdims=True)
        den = den + carried * jnp.sum(feat.astype(f32) * norm, axis=0, keepdims=True)
        num = dot(v[:, rows], weight.astype(bf16), 0, 0)
        num = num + carried * dot(state_of(near, far, keep, h), feat, 0, 0)
        y = num / den
        quotient[rows] = y
        att[rows] = y.astype(bf16)
        dens[h : h + 1] = den
    dens[HEADS:] = jnp.ones((8 - HEADS, TOK), f32)


def shard_of(ids, k):
    return lax.rem(ids[3] + k + 8, 8)


def partial_terms(count, ids, att, *refs):
    parts, (send, keep) = refs[: 2 * count], refs[2 * count :]
    first = ids[2] == 0
    half = TOK // 2
    for n in range(count):
        both = dot(att[:, :half], parts[2 * n][...], 1, 0)
        both = (both + dot(att[:, half:], parts[2 * n + 1][...], 1, 0)).astype(bf16)
        for j in range(2):
            even = both[:, 256 * j : 256 * j + HEAD]
            odd = both[:, 256 * j + HEAD : 256 * (j + 1)]
            send[2 * n + j] = jnp.where(first, odd, even)
            keep[2 * n + j] = jnp.where(first, even, odd)


def sum_cores(firsts, count, ids, *refs):
    outs, whole = refs[2 * count : -1], refs[-1]
    at = 0
    for group in range(count):
        keep, got = refs[group], refs[count + group]
        for n in range(keep.shape[0]):
            whole[at] = (keep[n].astype(f32) + got[n].astype(f32)).astype(bf16)
            at += 1
    for d in range(4):
        x = lax.rem(ids[5] + d, 4)
        for pair, k in enumerate(firsts):
            other = (lax.rem(shard_of(ids, k), 2) != x // 2).astype(jnp.int32)
            outs[d][pair] = whole[4 * pair + 2 * other + lax.rem(x, 2)]


def add_up(refs, *at):
    total = refs[0][at].astype(f32)
    for ref in refs[1:]:
        total = total + ref[at].astype(f32)
    return total


def sum_along_x(ids, *refs):
    ins, outs, whole = refs[:8], refs[8:12], refs[12]
    for group, places in enumerate(((0, 3), (1, 2))):
        for pair, slot in enumerate(places):
            whole[slot] = add_up(ins[4 * group : 4 * group + 4], pair)
    for d in range(4):
        shard = 2 * lax.rem(ids[4] + d, 4) + ids[5] // 2
        slot = lax.rem(shard - ids[3] + 8, 8) // 2
        outs[d][...] = whole[slot].astype(outs[d].dtype)


def sum_along_y(own, a, b, c, out):
    out[...] = add_up((own, a, b, c), Ellipsis)


def upstream(order, ids, w, *refs):
    parts, up = refs[:-1], refs[-1]
    half = TOK // 2
    for p in range(2):
        total = jnp.zeros((TOK, half), f32)
        for n, k in enumerate(order):
            at = pl.multiple_of(shard_of(ids, k) * TOK, TOK)
            total = total + dot(w[:, pl.ds(at, TOK)], parts[2 * n + p][...], 1, 1)
        up[:, half * p : half * (p + 1)] = total


def local_adjoint(up, quotient, dens, qkt, aux, pick, cols, ng, dg, out):
    carried = aux[2:3]
    table, column = pick[...], cols[...]
    norms = []
    for h in range(HEADS):
        rows = slice(HEAD * h, HEAD * (h + 1))
        inv = 1.0 / dens[h : h + 1]
        upstream = up[rows]
        den_grad = -jnp.sum(upstream * quotient[rows], axis=0, keepdims=True) * inv
        num_grad = (upstream * inv).astype(bf16)
        ng[rows] = num_grad
        dg[h : h + 1] = den_grad
        feat = lifted(table, column, qkt[32 * h : 32 * h + QK])[2]
        feat = feat.astype(f32) * carried
        norms.append(jnp.sum(feat * den_grad, axis=1, keepdims=True) * column[:, 3:4])
        out[h] = (dot(feat.astype(bf16), num_grad, 1, 1) * column[:, 3:4]).astype(bf16)
    dg[HEADS:] = jnp.zeros((8 - HEADS, TOK), f32)
    put_norms(out, norms)


def local_grads(ng, dg, qkt, v, aux, pick, pick_t, cols, near, far, qkg, vg):
    keep = aux[4:5, 0:1]
    carried = aux[2:3]
    table, column = pick[...], cols[...]
    for h in range(HEADS):
        rows = slice(HEAD * h, HEAD * (h + 1))
        q, k = qkt[32 * h : 32 * h + QK], qkt[32 * h + QK : 32 * h + 2 * QK]
        scores, visible, weight = scores_of(qkt, aux, h)
        num_grad, den_grad = ng[rows], dg[h : h + 1]
        mix = dot(v[:, rows], num_grad, 1, 0) + den_grad
        score_grad = jnp.where(visible, mix * (1.0 + scores), 0.0).astype(bf16)
        vg[:, rows] = dot(weight.astype(bf16), num_grad, 1, 1)
        a, b, _ = lifted(table, column, q)
        g = dot(state_of(near, far, keep, h), num_grad, 1, 0)
        g = carried * (g + norm_of(near, far, keep, h) * den_grad)
        qkg[32 * h : 32 * h + QK] = 0.25 * dot(k, score_grad, 1, 0) + chain(
            pick_t[...], column, g, a, b
        )
        qkg[32 * h + QK : 32 * h + 2 * QK] = 0.25 * dot(q, score_grad, 1, 1)


def finish(qkg, vg, qkt, v, aux, pick, pick_t, cols, near, far, qk_out, v_out, acc):
    keep = aux[5:6, 0:1]
    ending = aux[1:2]
    table, column = pick[...], cols[...]
    for h in range(HEADS):
        rows = slice(HEAD * h, HEAD * (h + 1))
        a, b, feat = lifted(table, column, qkt[32 * h + QK : 32 * h + 2 * QK])
        feat = (feat.astype(f32) * ending).astype(bf16)
        adjoint = state_of(near, far, keep, h)
        v_out[:, rows] = (vg[:, rows] + dot(feat, adjoint, 0, 0)).astype(bf16)
        g = dot(adjoint, v[:, rows], 1, 1) + norm_of(near, far, keep, h)
        acc[32 * h : 32 * h + QK] = qkg[32 * h : 32 * h + QK]
        acc[32 * h + QK : 32 * h + 2 * QK] = qkg[32 * h + QK : 32 * h + 2 * QK] + chain(
            pick_t[...], column, g * ending, a, b
        )
    qk_out[...] = acc[...].T.astype(bf16)


def on_device(query_key, values, out_grad, out_weight, doc_lengths):
    c = lax.axis_index("ctx").astype(jnp.int32)
    ids = jnp.stack([c * TOK, c // 2, c % 2, lax.axis_index("head").astype(jnp.int32), c // 8, (c // 2) % 4])
    np_pick, np_pick_t, np_cols = feature_tables()
    pick, pick_t, cols = jnp.asarray(np_pick, bf16), jnp.asarray(np_pick_t, bf16), jnp.asarray(np_cols)
    slab = ((HEADS + 1, FEAT, HEAD), bf16)

    half = TOK // 2
    own = lax.optimization_barrier([out_grad[:half], out_grad[half:]])
    query_key, own[0] = lax.optimization_barrier((query_key, own[0]))
    local, qkt, aux = call(
        local_state,
        [slab, ((128, TOK), bf16), ((8, TOK), f32)],
        5,
        2**27,
        2**21,
        limit=56 * MIB,
    )(ids, doc_lengths.reshape(1, 128), query_key, values, pick, cols)

    later, aux = lax.optimization_barrier((own[1], aux))
    own = [own[0], later]
    pieces = {0: own}
    ring = {d: [(i, (i + d) % 8) for i in range(8)] for d in (1, -1)}
    for step in range(1, 4):
        for d in (1, -1):
            before = pieces[-d * (step - 1)]
            pieces[-d * step] = [lax.ppermute(x, "head", ring[d]) for x in before]
    pieces[4] = [lax.ppermute(pieces[-3][0], "head", ring[1]), lax.ppermute(pieces[3][1], "head", ring[-1])]

    def exchange(mine, sign):
        got = lax.ppermute(mine, "ctx", shift(sign))
        pair = call(pair_sum, [slab], 3, 2**20, 2**20, False)(mine, got, aux)[0]
        return lax.ppermute(pair, "ctx", shift(sign)), lax.ppermute(pair, "ctx", shift(3 * sign))

    near, far = exchange(local, 1)
    att, quotient, dens = call(
        attend,
        [((TOK, TOK), bf16), ((TOK, TOK), f32), ((8, TOK), f32)],
        7,
        2**30,
        4 * 2**20,
        False,
    )(qkt, values, aux, pick, cols, near, far)

    send = lambda x, pairs: lax.ppermute(x, "ctx", pairs)

    def terms(shards):
        n = len(shards)
        block = ((2 * n, TOK, HEAD), bf16)
        out, keep = call(
            functools.partial(partial_terms, n), [block, block], 1 + 2 * n, n * 2**28, 2**20 * n
        )(ids, att, *[x for k in shards for x in pieces[k]])
        return keep, send(out, [(i, i ^ 1) for i in range(32)])

    def spread(firsts, found):
        count = len(found)
        parts = pl.pallas_call(
            functools.partial(sum_cores, firsts, count),
            out_shape=[jax.ShapeDtypeStruct((2, TOK, HEAD), bf16)] * 4,
            in_specs=[pl.BlockSpec(memory_space=pltpu.SMEM)]
            + [pl.BlockSpec(memory_space=pltpu.VMEM)] * (2 * count),
            out_specs=[pl.BlockSpec(memory_space=pltpu.VMEM)] * 4,
            scratch_shapes=[pltpu.VMEM((8, TOK, HEAD), bf16)],
            compiler_params=pltpu.CompilerParams(vmem_limit_bytes=LIMIT),
            cost_estimate=pl.CostEstimate(flops=2**20, bytes_accessed=2**21, transcendentals=0),
        )(ids, *[f[0] for f in found], *[f[1] for f in found])
        return [parts[0]] + [send(parts[d], along(0, d)) for d in (1, 3, 2)]

    steps = [(0, 1, -2, -1), (2, 3, 4, -3)]
    early = spread((0, -2), [terms((0, 1, -2, -1))])
    middle, late = terms((2, 3)), terms((4, -3))

    order = [k for shards in steps for k in shards]
    up = call(functools.partial(upstream, order), [((TOK, TOK), f32)], 17, 2**32, 9 * 2**20)(
        ids, out_weight, *[x for k in order for x in pieces[k]]
    )[0]

    ng, dg, adj_local = call(
        local_adjoint,
        [((TOK, TOK), bf16), ((8, TOK), f32), slab],
        7,
        2**28,
        4 * 2**20,
        False,
    )(up, quotient, dens, qkt, aux, pick, cols)
    adj_near, adj_far = exchange(adj_local, -1)
    kept, adj_local = lax.optimization_barrier((late[0], adj_local))
    rest = spread((2, 4), [middle, (kept, late[1])])
    qkg, vg = call(
        local_grads, [((128, TOK), f32), ((TOK, TOK), f32)], 10, 2**31, 4 * 2**20, False
    )(ng, dg, qkt, values, aux, pick, pick_t, cols, near, far)
    rest[0], vg = lax.optimization_barrier((rest[0], vg))
    sums = pl.pallas_call(
        sum_along_x,
        out_shape=[jax.ShapeDtypeStruct((TOK, HEAD), bf16 if d else f32) for d in range(4)],
        in_specs=[pl.BlockSpec(memory_space=pltpu.SMEM)]
        + [pl.BlockSpec(memory_space=pltpu.VMEM)] * 8,
        out_specs=[pl.BlockSpec(memory_space=pltpu.VMEM)] * 4,
        scratch_shapes=[pltpu.VMEM((4, TOK, HEAD), f32)],
        compiler_params=pltpu.CompilerParams(vmem_limit_bytes=LIMIT),
        cost_estimate=pl.CostEstimate(flops=2**20, bytes_accessed=2**21, transcendentals=0),
    )(ids, *early, *rest)
    across = [send(sums[d], along(d, 0)) for d in (1, 3, 2)]
    proj_grad = call(sum_along_y, [((TOK, HEAD), f32)], 4, 2**19, 2**20, False)(
        sums[0], *across
    )[0]
    qk_grad, value_grad = pl.pallas_call(
        finish,
        out_shape=[
            jax.ShapeDtypeStruct((TOK, 128), bf16),
            jax.ShapeDtypeStruct((TOK, TOK), bf16),
        ],
        in_specs=[pl.BlockSpec(memory_space=pltpu.VMEM)] * 10,
        out_specs=[pl.BlockSpec(memory_space=pltpu.VMEM)] * 2,
        scratch_shapes=[pltpu.VMEM((128, TOK), f32)],
        compiler_params=pltpu.CompilerParams(vmem_limit_bytes=LIMIT),
        cost_estimate=pl.CostEstimate(flops=2**29, bytes_accessed=4 * 2**20, transcendentals=0),
    )(qkg, vg, qkt, values, aux, pick, pick_t, cols, adj_near, adj_far)
    return (qk_grad, value_grad, proj_grad)


def solution(mesh):
    placed = (P("ctx", "head"), P("ctx", "head"), P("ctx", "head"), P("head", None), P())
    return jax.shard_map(
        on_device,
        mesh=mesh,
        in_specs=placed,
        out_specs=(P("ctx", "head"), P("ctx", "head"), P("head", "ctx")),
        check_vma=False,
    )
```

```python
import functools
import math

import jax
import jax.numpy as jnp
import numpy as np
from jax import lax
from jax.experimental import pallas as pl
from jax.experimental.pallas import tpu as pltpu
from jax.sharding import PartitionSpec as P

HEAD = 128
QK = 16
HEADS = 4
TOK = 512
FEAT = 160
QUAD = 0.25 / math.sqrt(2.0)
bf16 = jnp.bfloat16
f32 = jnp.float32
MIB = 1024 * 1024
LIMIT = 20 * MIB


def feature_tables():
    pairs = [(a, b) for a in range(QK) for b in range(a, QK)]
    pick = np.zeros((FEAT, 2 * QK), np.float32)
    cols = np.zeros((FEAT, HEAD), np.float32)
    cols[0, :4] = (1.0, 1.0, 1.0, 1.0)
    for a in range(QK):
        pick[1 + a, a] = 1.0
        cols[1 + a, :4] = (0.0, 1.0, 0.5, 1.0)
    for n, (a, b) in enumerate(pairs):
        row = 1 + QK + n
        pick[row, a] = 1.0
        pick[row, QK + b] = 1.0
        cols[row, :4] = (0.0, 0.0, QUAD, 1.0 if a == b else 2.0)
    return pick, pick.T.copy(), cols


def place(i):
    return i // 8, (i // 2) % 4, i % 2


def index(y, x, k):
    return ((y % 4) * 4 + x % 4) * 2 + k


def along(dy, dx):
    return [(i, index(place(i)[0] + dy, place(i)[1] + dx, i % 2)) for i in range(32)]


def shift(k):
    return [(i, i + k) for i in range(32) if 0 <= i + k < 32]


def dot(a, b, ca, cb):
    return lax.dot_general(a, b, (((ca,), (cb,)), ((), ())), preferred_element_type=f32)


def call(body, outs, n_in, flops, nbytes, scalar=True, limit=LIMIT):
    specs = [pl.BlockSpec(memory_space=pltpu.VMEM)] * n_in
    if scalar:
        specs = [pl.BlockSpec(memory_space=pltpu.SMEM)] + specs
    return pl.pallas_call(
        body,
        out_shape=[jax.ShapeDtypeStruct(s, t) for s, t in outs],
        in_specs=specs,
        out_specs=[pl.BlockSpec(memory_space=pltpu.VMEM)] * len(outs),
        compiler_params=pltpu.CompilerParams(vmem_limit_bytes=limit),
        cost_estimate=pl.CostEstimate(flops=flops, bytes_accessed=nbytes, transcendentals=0),
    )


def lifted(pick, cols, x):
    a = dot(pick[:, :QK], x, 1, 0) + cols[:, 0:1]
    b = dot(pick[:, QK : 2 * QK], x, 1, 0) + cols[:, 1:2]
    return a, b, ((a * b) * cols[:, 2:3]).astype(bf16)


def split(x):
    high = x.astype(bf16)
    return high, (x - high.astype(f32)).astype(bf16)


def chain(pick_t, cols, g, a, b):
    scaled = g * cols[:, 2:3]
    out = jnp.zeros((QK, TOK), f32)
    for table, other in ((pick_t[:QK], b), (pick_t[QK : 2 * QK], a)):
        high, low = split(scaled * other)
        out = out + dot(table, high, 1, 0) + dot(table, low, 1, 0)
    return out


def put_norms(ref, norms):
    lane = lax.broadcasted_iota(jnp.int32, (FEAT, HEAD), 1)
    total = jnp.zeros((FEAT, HEAD), f32)
    for h in range(HEADS):
        high, low = split(norms[h])
        total = jnp.where(lane == h, high.astype(f32), total)
        total = jnp.where(lane == HEADS + h, low.astype(f32), total)
    ref[HEADS] = total.astype(bf16)


def norm_of(near, far, keep, h):
    def one(ref):
        part = ref[HEADS].astype(f32)
        return part[:, h : h + 1] + part[:, HEADS + h : HEADS + h + 1]

    return one(near) + keep * one(far)


def state_of(near, far, keep, h):
    return (near[h].astype(f32) + keep * far[h].astype(f32)).astype(bf16)


def local_state(ids, lens, qk, v, pick, cols, out, qkt, aux):
    off = ids[0].astype(f32)
    length = lens[...].astype(f32)
    later = lax.broadcasted_iota(jnp.int32, (128, 128), 1) < lax.broadcasted_iota(
        jnp.int32, (128, 128), 0
    )
    first = jnp.sum(jnp.where(later, length, 0.0), axis=1, keepdims=True) - off

    def doc_at(where_to):
        return jnp.max(jnp.where(first <= where_to, first, -1e9), axis=0, keepdims=True)

    start = doc_at(lax.broadcasted_iota(jnp.int32, (128, TOK), 1).astype(f32))
    last, prev, far = doc_at(TOK - 1.0), doc_at(-1.0), doc_at(3 * TOK - 1.0)
    ending = (start == last).astype(f32)
    aux[0:1] = start
    aux[1:2] = ending
    aux[2:3] = (start < 0.0).astype(f32)
    aux[3:4] = jnp.broadcast_to((last < 0.0).astype(f32), (1, TOK))
    aux[4:5] = jnp.broadcast_to((prev < -2.0 * TOK).astype(f32), (1, TOK))
    aux[5:6] = jnp.broadcast_to((far < 1.0 * TOK).astype(f32), (1, TOK))
    aux[6:8] = jnp.zeros((2, TOK), f32)
    qkt[...] = qk[...].astype(f32).T.astype(bf16)
    norms = []
    table, column = pick[...], cols[...]
    for h in range(HEADS):
        feat = lifted(table, column, qkt[32 * h + QK : 32 * h + 2 * QK])[2]
        feat = jnp.where(ending > 0.5, feat.astype(f32), 0.0)
        norms.append(jnp.sum(feat, axis=1, keepdims=True) * column[:, 3:4])
        state = dot(feat.astype(bf16), v[:, HEAD * h : HEAD * (h + 1)], 1, 0)
        out[h] = (state * column[:, 3:4]).astype(bf16)
    put_norms(out, norms)


def pair_sum(own, got, aux, out):
    keep = aux[3:4, 0:1]
    for h in range(HEADS):
        out[h] = (own[h].astype(f32) + keep * got[h].astype(f32)).astype(bf16)
    put_norms(out, [norm_of(own, got, keep, h) for h in range(HEADS)])


def scores_of(qkt, aux, h):
    q, k = qkt[32 * h : 32 * h + QK], qkt[32 * h + QK : 32 * h + 2 * QK]
    scores = dot(k, q, 0, 0) * 0.25
    row = lax.broadcasted_iota(jnp.int32, (TOK, TOK), 0)
    col = lax.broadcasted_iota(jnp.int32, (TOK, TOK), 1)
    visible = (row >= aux[0:1].astype(jnp.int32)) & (row <= col)
    return scores, visible, jnp.where(visible, 1.0 + scores + 0.5 * scores * scores, 0.0)


def attend(qkt, v, aux, pick, cols, near, far, att, quotient, dens):
    keep = aux[4:5, 0:1]
    carried = aux[2:3]
    table, column = pick[...], cols[...]
    for h in range(HEADS):
        rows = slice(HEAD * h, HEAD * (h + 1))
        weight = scores_of(qkt, aux, h)[2]
        feat = lifted(table, column, qkt[32 * h : 32 * h + QK])[2]
        norm = norm_of(near, far, keep, h)
        den = jnp.sum(weight, axis=0, keepdims=True)
        den = den + carried * jnp.sum(feat.astype(f32) * norm, axis=0, keepdims=True)
        num = dot(v[:, rows], weight.astype(bf16), 0, 0)
        num = num + carried * dot(state_of(near, far, keep, h), feat, 0, 0)
        y = num / den
        quotient[rows] = y
        att[rows] = y.astype(bf16)
        dens[h : h + 1] = den
    dens[HEADS:] = jnp.ones((8 - HEADS, TOK), f32)


def shard_of(ids, k):
    return lax.rem(ids[3] + k + 8, 8)


def partial_terms(count, ids, att, *refs):
    parts, (send, keep) = refs[: 2 * count], refs[2 * count :]
    first = ids[2] == 0
    half = TOK // 2
    for n in range(count):
        both = dot(att[:, :half], parts[2 * n][...], 1, 0)
        both = (both + dot(att[:, half:], parts[2 * n + 1][...], 1, 0)).astype(bf16)
        for j in range(2):
            even = both[:, 256 * j : 256 * j + HEAD]
            odd = both[:, 256 * j + HEAD : 256 * (j + 1)]
            send[2 * n + j] = jnp.where(first, odd, even)
            keep[2 * n + j] = jnp.where(first, even, odd)


def sum_cores(firsts, count, ids, *refs):
    outs, whole = refs[2 * count : -1], refs[-1]
    at = 0
    for group in range(count):
        keep, got = refs[group], refs[count + group]
        for n in range(keep.shape[0]):
            whole[at] = (keep[n].astype(f32) + got[n].astype(f32)).astype(bf16)
            at += 1
    for d in range(4):
        x = lax.rem(ids[5] + d, 4)
        for pair, k in enumerate(firsts):
            other = (lax.rem(shard_of(ids, k), 2) != x // 2).astype(jnp.int32)
            outs[d][pair] = whole[4 * pair + 2 * other + lax.rem(x, 2)]


def add_up(refs, *at):
    total = refs[0][at].astype(f32)
    for ref in refs[1:]:
        total = total + ref[at].astype(f32)
    return total


def sum_along_x(ids, *refs):
    ins, outs, whole = refs[:8], refs[8:12], refs[12]
    for group, places in enumerate(((0, 3), (1, 2))):
        for pair, slot in enumerate(places):
            whole[slot] = add_up(ins[4 * group : 4 * group + 4], pair)
    for d in range(4):
        shard = 2 * lax.rem(ids[4] + d, 4) + ids[5] // 2
        slot = lax.rem(shard - ids[3] + 8, 8) // 2
        outs[d][...] = whole[slot].astype(outs[d].dtype)


def sum_along_y(own, a, b, c, out):
    out[...] = add_up((own, a, b, c), Ellipsis)


def upstream(order, ids, w, *refs):
    parts, up = refs[:-1], refs[-1]
    half = TOK // 2
    for p in range(2):
        total = jnp.zeros((TOK, half), f32)
        for n, k in enumerate(order):
            at = pl.multiple_of(shard_of(ids, k) * TOK, TOK)
            total = total + dot(w[:, pl.ds(at, TOK)], parts[2 * n + p][...], 1, 1)
        up[:, half * p : half * (p + 1)] = total


def local_adjoint(up, quotient, dens, qkt, aux, pick, cols, ng, dg, out):
    carried = aux[2:3]
    table, column = pick[...], cols[...]
    norms = []
    for h in range(HEADS):
        rows = slice(HEAD * h, HEAD * (h + 1))
        inv = 1.0 / dens[h : h + 1]
        upstream = up[rows]
        den_grad = -jnp.sum(upstream * quotient[rows], axis=0, keepdims=True) * inv
        num_grad = (upstream * inv).astype(bf16)
        ng[rows] = num_grad
        dg[h : h + 1] = den_grad
        feat = lifted(table, column, qkt[32 * h : 32 * h + QK])[2]
        feat = feat.astype(f32) * carried
        norms.append(jnp.sum(feat * den_grad, axis=1, keepdims=True) * column[:, 3:4])
        out[h] = (dot(feat.astype(bf16), num_grad, 1, 1) * column[:, 3:4]).astype(bf16)
    dg[HEADS:] = jnp.zeros((8 - HEADS, TOK), f32)
    put_norms(out, norms)


def local_grads(ng, dg, qkt, v, aux, pick, pick_t, cols, near, far, qkg, vg):
    keep = aux[4:5, 0:1]
    carried = aux[2:3]
    table, column = pick[...], cols[...]
    for h in range(HEADS):
        rows = slice(HEAD * h, HEAD * (h + 1))
        q, k = qkt[32 * h : 32 * h + QK], qkt[32 * h + QK : 32 * h + 2 * QK]
        scores, visible, weight = scores_of(qkt, aux, h)
        num_grad, den_grad = ng[rows], dg[h : h + 1]
        mix = dot(v[:, rows], num_grad, 1, 0) + den_grad
        score_grad = jnp.where(visible, mix * (1.0 + scores), 0.0).astype(bf16)
        vg[:, rows] = dot(weight.astype(bf16), num_grad, 1, 1)
        a, b, _ = lifted(table, column, q)
        g = dot(state_of(near, far, keep, h), num_grad, 1, 0)
        g = carried * (g + norm_of(near, far, keep, h) * den_grad)
        qkg[32 * h : 32 * h + QK] = 0.25 * dot(k, score_grad, 1, 0) + chain(
            pick_t[...], column, g, a, b
        )
        qkg[32 * h + QK : 32 * h + 2 * QK] = 0.25 * dot(q, score_grad, 1, 1)


def finish(qkg, vg, qkt, v, aux, pick, pick_t, cols, near, far, qk_out, v_out, acc):
    keep = aux[5:6, 0:1]
    ending = aux[1:2]
    table, column = pick[...], cols[...]
    for h in range(HEADS):
        rows = slice(HEAD * h, HEAD * (h + 1))
        a, b, feat = lifted(table, column, qkt[32 * h + QK : 32 * h + 2 * QK])
        feat = (feat.astype(f32) * ending).astype(bf16)
        adjoint = state_of(near, far, keep, h)
        v_out[:, rows] = (vg[:, rows] + dot(feat, adjoint, 0, 0)).astype(bf16)
        g = dot(adjoint, v[:, rows], 1, 1) + norm_of(near, far, keep, h)
        acc[32 * h : 32 * h + QK] = qkg[32 * h : 32 * h + QK]
        acc[32 * h + QK : 32 * h + 2 * QK] = qkg[32 * h + QK : 32 * h + 2 * QK] + chain(
            pick_t[...], column, g * ending, a, b
        )
    qk_out[...] = acc[...].T.astype(bf16)


def on_device(query_key, values, out_grad, out_weight, doc_lengths):
    c = lax.axis_index("ctx").astype(jnp.int32)
    ids = jnp.stack([c * TOK, c // 2, c % 2, lax.axis_index("head").astype(jnp.int32), c // 8, (c // 2) % 4])
    np_pick, np_pick_t, np_cols = feature_tables()
    pick, pick_t, cols = jnp.asarray(np_pick, bf16), jnp.asarray(np_pick_t, bf16), jnp.asarray(np_cols)
    slab = ((HEADS + 1, FEAT, HEAD), bf16)

    half = TOK // 2
    own = lax.optimization_barrier([out_grad[:half], out_grad[half:]])
    query_key, own[0] = lax.optimization_barrier((query_key, own[0]))
    local, qkt, aux = call(
        local_state,
        [slab, ((128, TOK), bf16), ((8, TOK), f32)],
        5,
        2**27,
        2**21,
        limit=56 * MIB,
    )(ids, doc_lengths.reshape(1, 128), query_key, values, pick, cols)

    later, aux = lax.optimization_barrier((own[1], aux))
    own = [own[0], later]
    pieces = {0: own}
    ring = {d: [(i, (i + d) % 8) for i in range(8)] for d in (1, -1)}
    for step in range(1, 4):
        for d in (1, -1):
            before = pieces[-d * (step - 1)]
            pieces[-d * step] = [lax.ppermute(x, "head", ring[d]) for x in before]
    pieces[4] = [lax.ppermute(pieces[-3][0], "head", ring[1]), lax.ppermute(pieces[3][1], "head", ring[-1])]

    def exchange(mine, sign):
        got = lax.ppermute(mine, "ctx", shift(sign))
        pair = call(pair_sum, [slab], 3, 2**20, 2**20, False)(mine, got, aux)[0]
        return lax.ppermute(pair, "ctx", shift(sign)), lax.ppermute(pair, "ctx", shift(3 * sign))

    near, far = exchange(local, 1)
    att, quotient, dens = call(
        attend,
        [((TOK, TOK), bf16), ((TOK, TOK), f32), ((8, TOK), f32)],
        7,
        2**30,
        4 * 2**20,
        False,
    )(qkt, values, aux, pick, cols, near, far)

    send = lambda x, pairs: lax.ppermute(x, "ctx", pairs)

    def terms(shards):
        n = len(shards)
        block = ((2 * n, TOK, HEAD), bf16)
        out, keep = call(
            functools.partial(partial_terms, n), [block, block], 1 + 2 * n, n * 2**28, 2**20 * n
        )(ids, att, *[x for k in shards for x in pieces[k]])
        return keep, send(out, [(i, i ^ 1) for i in range(32)])

    def spread(firsts, found):
        count = len(found)
        parts = pl.pallas_call(
            functools.partial(sum_cores, firsts, count),
            out_shape=[jax.ShapeDtypeStruct((2, TOK, HEAD), bf16)] * 4,
            in_specs=[pl.BlockSpec(memory_space=pltpu.SMEM)]
            + [pl.BlockSpec(memory_space=pltpu.VMEM)] * (2 * count),
            out_specs=[pl.BlockSpec(memory_space=pltpu.VMEM)] * 4,
            scratch_shapes=[pltpu.VMEM((8, TOK, HEAD), bf16)],
            compiler_params=pltpu.CompilerParams(vmem_limit_bytes=LIMIT),
            cost_estimate=pl.CostEstimate(flops=2**20, bytes_accessed=2**21, transcendentals=0),
        )(ids, *[f[0] for f in found], *[f[1] for f in found])
        return [parts[0]] + [send(parts[d], along(0, d)) for d in (2, 1, 3)]

    steps = [(0, 1, -2, -1), (2, 3, 4, -3)]
    early = spread((0, -2), [terms((0, 1, -2, -1))])
    middle, late = terms((2, 3)), terms((4, -3))

    order = [k for shards in steps for k in shards]
    up = call(functools.partial(upstream, order), [((TOK, TOK), f32)], 17, 2**32, 9 * 2**20)(
        ids, out_weight, *[x for k in order for x in pieces[k]]
    )[0]

    ng, dg, adj_local = call(
        local_adjoint,
        [((TOK, TOK), bf16), ((8, TOK), f32), slab],
        7,
        2**28,
        4 * 2**20,
        False,
    )(up, quotient, dens, qkt, aux, pick, cols)
    adj_near, adj_far = exchange(adj_local, -1)
    kept, adj_local = lax.optimization_barrier((late[0], adj_local))
    rest = spread((2, 4), [middle, (kept, late[1])])
    qkg, vg = call(
        local_grads, [((128, TOK), f32), ((TOK, TOK), f32)], 10, 2**31, 4 * 2**20, False
    )(ng, dg, qkt, values, aux, pick, pick_t, cols, near, far)
    rest[0], vg = lax.optimization_barrier((rest[0], vg))
    sums = pl.pallas_call(
        sum_along_x,
        out_shape=[jax.ShapeDtypeStruct((TOK, HEAD), bf16 if d else f32) for d in range(4)],
        in_specs=[pl.BlockSpec(memory_space=pltpu.SMEM)]
        + [pl.BlockSpec(memory_space=pltpu.VMEM)] * 8,
        out_specs=[pl.BlockSpec(memory_space=pltpu.VMEM)] * 4,
        scratch_shapes=[pltpu.VMEM((4, TOK, HEAD), f32)],
        compiler_params=pltpu.CompilerParams(vmem_limit_bytes=LIMIT),
        cost_estimate=pl.CostEstimate(flops=2**20, bytes_accessed=2**21, transcendentals=0),
    )(ids, *early, *rest)
    across = [send(sums[d], along(d, 0)) for d in (2, 1, 3)]
    proj_grad = call(sum_along_y, [((TOK, HEAD), f32)], 4, 2**19, 2**20, False)(
        sums[0], *across
    )[0]
    qk_grad, value_grad = pl.pallas_call(
        finish,
        out_shape=[
            jax.ShapeDtypeStruct((TOK, 128), bf16),
            jax.ShapeDtypeStruct((TOK, TOK), bf16),
        ],
        in_specs=[pl.BlockSpec(memory_space=pltpu.VMEM)] * 10,
        out_specs=[pl.BlockSpec(memory_space=pltpu.VMEM)] * 2,
        scratch_shapes=[pltpu.VMEM((128, TOK), f32)],
        compiler_params=pltpu.CompilerParams(vmem_limit_bytes=LIMIT),
        cost_estimate=pl.CostEstimate(flops=2**29, bytes_accessed=4 * 2**20, transcendentals=0),
    )(qkg, vg, qkt, values, aux, pick, pick_t, cols, adj_near, adj_far)
    return (qk_grad, value_grad, proj_grad)


def solution(mesh):
    placed = (P("ctx", "head"), P("ctx", "head"), P("ctx", "head"), P("head", None), P())
    return jax.shard_map(
        on_device,
        mesh=mesh,
        in_specs=placed,
        out_specs=(P("ctx", "head"), P("ctx", "head"), P("head", "ctx")),
        check_vma=False,
    )
```
